32 devices in a mesh: grp: 2 (over y), feat: 4 (over z), layer: 2 (over x), dec: 2 (over core).
Axes of the slice: x: 2, y: 2, z: 4, core: 2. Of those that a mesh axis runs over, the one named last changes fastest.
Arguments:
- clean_resid: bfloat16 [2, 224, 2304], P('layer', ('grp', 'feat', 'dec')), parts along dimension 1, may hold values from -6 to 6
- corrupt_resid: bfloat16 [2, 224, 2304], P('layer', ('grp', 'feat', 'dec')), parts along dimension 1, may hold values from -6 to 6
- enc_weight: bfloat16 [2, 2304, 2048], P('layer', None, ('feat', 'dec')), may hold values from -0.125 to 0.125
- enc_bias: float32 [2, 2048], P('layer', ('feat', 'dec')), may hold values from -0.8 to 0.4
- dec_weight: bfloat16 [2, 3, 2048, 2304], P('layer', None, ('feat', 'dec')), may hold values from -0.078125 to 0.078125
- dec_bias: float32 [2, 2304], P('layer'), may hold values from -3 to 3
- patch_index: int32 [2, 8, 16], P('layer', ('feat', 'dec')), may hold values from 0 to 255, as said below
Outputs:
- recon: bfloat16 [2, 224, 2304], P('layer', ('grp', 'feat', 'dec')), parts along dimension 1
The draws below stay inside these ranges and needn't reach their ends.
There are 2 independent parts, one for each index of `grp`. The reference program is written for one: setup_inputs(seed, part) draws one part's arguments, and reference() takes and returns one part's arrays. A program takes and returns all parts, laid end to end along the dimension named above; an argument that names none is the same for every part. Nothing has to cross between parts.
Inputs may be any that keep to these rules, and one draw needn't show every extreme that they name: `patch_index`: for each layer and slab, 16 different feature numbers within the slab.
All inputs are finite; a program needn't handle non-finite values.
Results may differ from the reference program's by a relative error of at most 0.0043.
Values may be sent and summed in bfloat16 or wider, within the bound.
No kernel may reach another device: no remote copies, remote signals or barrier semaphores. Data moves between devices by JAX's collectives and lax.ppermute only.
A program may use at most 64 MiB of HBM per device.

```python
import jax
import jax.numpy as jnp

D = 2304
FS = 256
KP = 16
REACH = 3
LAYERS = 2
SLABS = 8
FEATS = 2048
TOKENS = 112


def draw_patch_index(key, part):
    keys = jax.random.split(key, LAYERS * SLABS)
    orders = jax.vmap(lambda single: jax.random.permutation(single, FS))(keys).astype(jnp.int32)
    high_pos = jnp.argmax(orders[0] == FS - 1)
    orders = orders.at[0].set(jnp.roll(orders[0], -high_pos))
    if LAYERS * SLABS > 1:
        low_pos = jnp.argmax(orders[1] == 0)
        orders = orders.at[1].set(jnp.roll(orders[1], -low_pos))
    return orders[:, :KP].reshape(LAYERS, SLABS, KP).astype(jnp.int32)


def block_scale(rng, dims, shards, smallest, largest):
    def one(axis_at, shards_of):
        heights = jax.random.uniform(jax.random.fold_in(jax.random.fold_in(rng, 6), axis_at), (shards_of,), jnp.float32, smallest / len(shards), largest / len(shards))
        return jnp.repeat(jnp.exp(heights), dims[axis_at] // shards_of).reshape((-1,) + (1,) * (len(dims) - axis_at - 1))

    gain = one(*shards[0])
    for cut in shards[1:]:
        gain = gain * one(*cut)
    return gain


def scatter_about(stream_key, extent, deviation, bound, shards=(), kind=jnp.bfloat16):
    result = jax.random.normal(stream_key, extent, jnp.float32) * deviation
    if len(shards) > 0:
        result = block_scale(stream_key, extent, shards, -0.22, 0.18) * result
    return jnp.clip(result, min=-bound, max=bound).astype(kind)


def setup_inputs(seed: int = 0, part: int = 0) -> dict:
    key_list = jax.random.split(jax.random.key(seed), 8)
    part_splits = jax.random.split(jax.random.fold_in(key_list[7], part), 8)
    clean_resid = scatter_about(part_splits[0], (LAYERS, TOKENS, D), 1.0, 6.0, ((0, 2), (1, 8)))
    corrupt_resid = scatter_about(part_splits[1], (LAYERS, TOKENS, D), 1.0, 6.0, ((0, 2), (1, 8)))
    enc_weight = scatter_about(key_list[2], (LAYERS, D, FEATS), D ** -0.5, 0.125, ((0, 2), (2, 8)))
    enc_bias = jnp.clip(-0.8 + 1.2 * jax.random.uniform(key_list[3], (LAYERS, FEATS), jnp.float32) ** block_scale(key_list[3], (LAYERS, FEATS), ((0, 2), (1, 8)), -0.2, 0.2), -0.8, 0.4)
    dec_weight = scatter_about(key_list[4], (LAYERS, REACH, FEATS, D), (REACH * FEATS) ** -0.5, 0.078125, ((0, 2), (2, 8)))
    dec_bias = scatter_about(key_list[5], (LAYERS, D), 0.5, 3.0, ((0, 2),), jnp.float32)
    patch_index = draw_patch_index(jax.random.fold_in(key_list[7], 71), part)
    return dict(clean_resid=clean_resid, corrupt_resid=corrupt_resid, enc_weight=enc_weight, enc_bias=enc_bias, dec_weight=dec_weight, dec_bias=dec_bias, patch_index=patch_index)


def reference(clean_resid, corrupt_resid, enc_weight, enc_bias, dec_weight, dec_bias, patch_index):
    iota = jnp.arange(FS, dtype=jnp.int32)
    features = []
    for layer_id in range(LAYERS):
        clean_pre = jnp.dot(clean_resid[layer_id], enc_weight[layer_id], preferred_element_type=jnp.float32) + enc_bias[layer_id]
        corrupt_pre = jnp.dot(corrupt_resid[layer_id], enc_weight[layer_id], preferred_element_type=jnp.float32) + enc_bias[layer_id]
        marked = jnp.any(patch_index[layer_id].astype(jnp.int32)[:, :, None] == iota[None, None, :], axis=1).reshape(FEATS)
        chosen = jnp.where(marked[None, :], jax.nn.relu(corrupt_pre), jax.nn.relu(clean_pre))
        features.append(chosen.astype(jnp.bfloat16))
    results = []
    for target in range(LAYERS):
        total = jnp.zeros((TOKENS, D), jnp.float32)
        for k in range(REACH):
            if target - k >= 0:
                total = total + jnp.dot(features[target - k], dec_weight[target, k], preferred_element_type=jnp.float32)
        total = total + dec_bias[target]
        results.append(total.astype(jnp.bfloat16))
    return jnp.stack(results)
```

```python
import jax
import jax.numpy as jnp
from jax import lax
from jax.sharding import PartitionSpec as P

REACH = 3


def moved(value, axis, pairs):
    return lax.ppermute(value, axis, pairs)


def shifted(value, axis, by):
    count = lax.axis_size(axis)
    return moved(value, axis, [(i, i + by) for i in range(count) if 0 <= i + by < count])


def rotated(value, axis, by):
    count = lax.axis_size(axis)
    return moved(value, axis, [(i, (i + by) % count) for i in range(count)])


def local(clean_resid, corrupt_resid, enc_weight, enc_bias, dec_weight, dec_bias, patch_index):
    chips = lax.axis_size("feat")
    cores = lax.axis_size("dec")
    depth = min(REACH - 1, lax.axis_size("layer") - 1)
    width = enc_weight.shape[2]
    rows, model = clean_resid.shape[1:]
    both = jnp.stack([clean_resid[0], corrupt_resid[0]])
    got = [both] + [rotated(both, "feat", k) for k in range(1, chips)]
    picks = patch_index[0, 0]
    mark = jnp.any(picks[:, None] == jnp.arange(width, dtype=jnp.int32)[None, :], axis=0)
    small = jnp.concatenate([enc_bias, mark.astype(jnp.float32)[None]], axis=0)
    smalls = [small] + [rotated(small, "dec", j) for j in range(1, cores)]
    encs = [enc_weight[0]] + [rotated(enc_weight[0], "dec", j) for j in range(1, cores)]
    decw = dec_weight[0, : depth + 1]
    decs = [decw] + [rotated(decw, "dec", j) for j in range(1, cores)]
    tokens = jnp.concatenate(got, axis=1)
    clean_all, corrupt_all = tokens[0], tokens[1]
    feats = []
    for w, s in zip(encs, smalls):
        c = jnp.dot(clean_all, w, preferred_element_type=jnp.float32)
        d = jnp.dot(corrupt_all, w, preferred_element_type=jnp.float32)
        pre = jnp.where(s[1][None] > 0.5, d, c) + s[0][None]
        feats.append(jax.nn.relu(pre).astype(jnp.bfloat16))
    stacked = jnp.concatenate(feats, axis=1)
    known = [stacked] + [shifted(stacked, "layer", o) for o in range(1, depth + 1)]
    total = 0.0
    for k in range(depth + 1):
        for j in range(cores):
            total = total + jnp.dot(
                known[k][:, j * width : (j + 1) * width],
                decs[j][k],
                preferred_element_type=jnp.float32,
            )
    summed = total[:rows]
    for k in range(1, chips):
        part = total[k * rows : (k + 1) * rows].astype(jnp.bfloat16)
        summed = summed + rotated(part, "feat", -k).astype(jnp.float32)
    return (summed + dec_bias).astype(jnp.bfloat16)[None]


def solution(mesh):
    placed = (
        P("layer", ("grp", "feat", "dec"), None),
        P("layer", ("grp", "feat", "dec"), None),
        P("layer", None, ("feat", "dec")),
        P("layer", ("feat", "dec")),
        P("layer", None, ("feat", "dec"), None),
        P("layer", None),
        P("layer", ("feat", "dec"), None),
    )
    return jax.shard_map(
        local,
        mesh=mesh,
        in_specs=placed,
        out_specs=P("layer", ("grp", "feat", "dec"), None),
        check_vma=False,
    )
```

```python
import functools

import jax
import jax.numpy as jnp
from jax import lax
from jax.experimental import pallas as pl
from jax.experimental.pallas import tpu as pltpu
from jax.sharding import PartitionSpec as P

REACH = 3
SLOT = 16
FIRST = 0
VMEM = pltpu.VMEM
LIMIT = 48 * 1024 * 1024


def shifted(value, axis, by):
    count = lax.axis_size(axis)
    return lax.ppermute(value, axis, [(i, i + by) for i in range(count) if 0 <= i + by < count])


def rotated(value, axis, by):
    count = lax.axis_size(axis)
    return lax.ppermute(value, axis, [(i, (i + by) % count) for i in range(count)])


def near(value):
    return pltpu.with_memory_space_constraint(value, VMEM)


def far(value):
    return pltpu.with_memory_space_constraint(value, pltpu.HBM)


def call(body, outs, spaces, args, scratch=(), flops=0, moved=0):
    return pl.pallas_call(
        body,
        out_shape=outs,
        in_specs=[pl.BlockSpec(memory_space=s) for s in spaces],
        out_specs=jax.tree.map(lambda _: pl.BlockSpec(memory_space=VMEM), outs),
        scratch_shapes=list(scratch),
        compiler_params=pltpu.CompilerParams(vmem_limit_bytes=LIMIT),
        cost_estimate=pl.CostEstimate(flops=flops, bytes_accessed=moved, transcendentals=0),
    )(*args)


def stack_body(clean, corrupt, bias, picks, both, small, bias_v, picks_s, sems):
    copies = [
        pltpu.make_async_copy(picks.at[0], picks_s, sems.at[0]),
        pltpu.make_async_copy(bias, bias_v, sems.at[1]),
        pltpu.make_async_copy(clean.at[0], both.at[0], sems.at[2]),
        pltpu.make_async_copy(corrupt.at[0], both.at[1], sems.at[3]),
    ]
    for c in copies:
        c.start()
    copies[0].wait()
    width = small.shape[1]
    lane = lax.broadcasted_iota(jnp.int32, (1, width), 1)
    mark = jnp.zeros((1, width), jnp.float32)
    for i in range(picks_s.shape[1]):
        mark = jnp.where(lane == picks_s[0, i], 1.0, mark)
    small[1:2, :] = mark
    copies[1].wait()
    small[0:1, :] = bias_v[...]
    copies[2].wait()
    copies[3].wait()


def load_body(levels, enc, dec, after, enc_out, dec_out, sems):
    copies = [pltpu.make_async_copy(enc.at[0], enc_out, sems.at[0])]
    copies += [
        pltpu.make_async_copy(dec.at[0, k], dec_out.at[k], sems.at[k + 1]) for k in range(levels)
    ]
    for c in copies:
        c.start()
    for c in copies:
        c.wait()


def encode_body(chips, cores, *refs):
    got, smalls, encs = refs[:chips], refs[chips : chips + cores], refs[chips + cores : chips + 2 * cores]
    out, x = refs[chips + 2 * cores :]
    rows = got[0].shape[1]
    half = chips * SLOT
    for k in range(chips):
        for c in range(2):
            x[c * half + k * SLOT : c * half + k * SLOT + rows, :] = got[k][c]
    width = encs[0].shape[1]
    for j in range(cores):
        h = jnp.dot(x[...], encs[j][...], preferred_element_type=jnp.float32)
        pre = jnp.where(smalls[j][1:2, :] > 0.5, h[half:], h[:half]) + smalls[j][0:1, :]
        out[:, j * width : (j + 1) * width] = jnp.maximum(pre, 0.0).astype(jnp.bfloat16)


def dots(feats, decs, level, cores):
    width = decs[0].shape[1]
    total = None
    for j in range(cores):
        one = jnp.dot(
            feats[:, j * width : (j + 1) * width],
            decs[j][level],
            preferred_element_type=jnp.float32,
        )
        total = one if total is None else total + one
    return total


def own_body(cores, feats, *refs):
    decs, out = refs[:cores], refs[cores]
    out[...] = dots(feats, decs, 0, cores)


def rest_body(chips, cores, depth, rows, base, bias, *refs):
    known, decs = refs[:depth], refs[depth : depth + cores]
    outs = refs[depth + cores :]
    total = base[...]
    for k in range(depth):
        total = total + dots(known[k], decs, k + 1, cores)
    outs[0][...] = total[:rows] + bias[...]
    for k in range(1, chips):
        outs[k][...] = total[k * SLOT : k * SLOT + rows].astype(jnp.bfloat16)


def sum_body(own, *refs):
    total = own[...]
    for r in refs[:-1]:
        total = total + r[...].astype(jnp.float32)
    refs[-1][0] = total.astype(jnp.bfloat16)


def local(clean_resid, corrupt_resid, enc_weight, enc_bias, dec_weight, dec_bias, patch_index):
    chips = lax.axis_size("feat")
    cores = lax.axis_size("dec")
    depth = min(REACH - 1, lax.axis_size("layer") - 1)
    width = enc_weight.shape[2]
    rows, model = clean_resid.shape[1:]
    bf16, f32 = jnp.bfloat16, jnp.float32
    any_, hbm, dma = pl.ANY, pltpu.HBM, pltpu.SemaphoreType.DMA

    both, small = call(
        stack_body,
        (VMEM((2, rows, model), bf16), VMEM((2, width), f32)),
        (hbm,) * 4,
        [far(v) for v in (clean_resid, corrupt_resid, enc_bias, patch_index)],
        (VMEM((1, width), f32), pltpu.SMEM(patch_index.shape[1:], jnp.int32), dma((4,))),
    )
    got = [rotated(both, "feat", k) for k in range(chips - 1, 0, -1)]
    smalls = [small] + [rotated(small, "dec", j) for j in range(1, cores)]
    enc, dec = call(
        functools.partial(load_body, depth + 1),
        (VMEM((model, width), bf16), VMEM((depth + 1, width, model), bf16)),
        (hbm, hbm, any_),
        (far(enc_weight), far(dec_weight), smalls[-1]),
        (dma((depth + 2,)),),
    )
    got = [both] + got[::-1]
    encs = [enc] + [rotated(enc_weight[0], "dec", j) for j in range(1, cores)]
    decs = [dec] + [rotated(dec_weight[0], "dec", j) for j in range(1, cores)]
    feats = call(
        functools.partial(encode_body, chips, cores),
        VMEM((chips * SLOT, cores * width), bf16),
        (VMEM,) * (chips + 2 * cores),
        [near(v) for v in (*got, *smalls, *encs)],
        (VMEM((2 * chips * SLOT, model), bf16),),
        flops=4 * chips * SLOT * model * width * cores,
        moved=cores * width * model * 2,
    )
    known = [shifted(feats, "layer", o) for o in range(1, depth + 1)]
    base = call(
        functools.partial(own_body, cores),
        VMEM((chips * SLOT, model), f32),
        (VMEM,) * (1 + cores),
        [near(v) for v in (feats, *decs)],
        flops=2 * chips * SLOT * model * width * cores,
        moved=cores * width * model * 2,
    )
    parts = call(
        functools.partial(rest_body, chips, cores, depth, rows),
        (VMEM((rows, model), f32),) + (VMEM((rows, model), bf16),) * (chips - 1),
        (VMEM,) * (2 + depth + cores),
        [near(v) for v in (base, dec_bias, *known, *decs)],
        flops=2 * chips * SLOT * model * width * cores * depth,
        moved=cores * width * model * 2 * depth,
    )
    back = [rotated(parts[k], "feat", -k) for k in range(1, chips)]
    return call(
        sum_body,
        jax.ShapeDtypeStruct((1, rows, model), bf16),
        (VMEM,) * chips,
        [near(v) for v in (parts[0], *back)],
    )


def solution(mesh):
    placed = (
        P("layer", ("grp", "feat", "dec"), None),
        P("layer", ("grp", "feat", "dec"), None),
        P("layer", None, ("feat", "dec")),
        P("layer", ("feat", "dec")),
        P("layer", None, ("feat", "dec"), None),
        P("layer", None),
        P("layer", ("feat", "dec"), None),
    )
    return jax.shard_map(
        local,
        mesh=mesh,
        in_specs=placed,
        out_specs=P("layer", ("grp", "feat", "dec"), None),
        check_vma=False,
    )
```

```python
import functools

import jax
import jax.numpy as jnp
from jax import lax
from jax.experimental import pallas as pl
from jax.experimental.pallas import tpu as pltpu
from jax.sharding import PartitionSpec as P

REACH = 3
SLOT = 16
FIRST = 0
VMEM = pltpu.VMEM
LIMIT = 48 * 1024 * 1024


def shifted(value, axis, by):
    count = lax.axis_size(axis)
    return lax.ppermute(value, axis, [(i, i + by) for i in range(count) if 0 <= i + by < count])


def rotated(value, axis, by):
    count = lax.axis_size(axis)
    return lax.ppermute(value, axis, [(i, (i + by) % count) for i in range(count)])


def near(value):
    return pltpu.with_memory_space_constraint(value, VMEM)


def far(value):
    return pltpu.with_memory_space_constraint(value, pltpu.HBM)


def call(body, outs, spaces, args, scratch=(), flops=0, moved=0):
    return pl.pallas_call(
        body,
        out_shape=outs,
        in_specs=[pl.BlockSpec(memory_space=s) for s in spaces],
        out_specs=jax.tree.map(lambda _: pl.BlockSpec(memory_space=VMEM), outs),
        scratch_shapes=list(scratch),
        compiler_params=pltpu.CompilerParams(vmem_limit_bytes=LIMIT),
        cost_estimate=pl.CostEstimate(flops=flops, bytes_accessed=moved, transcendentals=0),
    )(*args)


def stack_body(clean, corrupt, both, sems):
    copies = [
        pltpu.make_async_copy(clean.at[0], both.at[0], sems.at[0]),
        pltpu.make_async_copy(corrupt.at[0], both.at[1], sems.at[1]),
    ]
    for c in copies:
        c.start()
    for c in copies:
        c.wait()


def load_body(levels, enc, dec, bias, picks, after, enc_out, dec_out, small, bias_v, picks_s, sems):
    copies = [
        pltpu.make_async_copy(picks.at[0], picks_s, sems.at[0]),
        pltpu.make_async_copy(bias, bias_v, sems.at[1]),
        pltpu.make_async_copy(enc.at[0], enc_out, sems.at[2]),
    ]
    copies += [
        pltpu.make_async_copy(dec.at[0, k], dec_out.at[k], sems.at[k + 3]) for k in range(levels)
    ]
    for c in copies:
        c.start()
    copies[0].wait()
    width = small.shape[1]
    lane = lax.broadcasted_iota(jnp.int32, (1, width), 1)
    mark = jnp.zeros((1, width), jnp.float32)
    for i in range(picks_s.shape[1]):
        mark = jnp.where(lane == picks_s[0, i], 1.0, mark)
    small[1:2, :] = mark
    copies[1].wait()
    small[0:1, :] = bias_v[...]
    for c in copies[2:]:
        c.wait()


def encode_body(chips, cores, *refs):
    got, smalls, encs = refs[:chips][::-1], refs[chips : chips + cores], refs[chips + cores : chips + 2 * cores]
    out, x = refs[chips + 2 * cores :]
    rows = got[0].shape[1]
    half = chips * SLOT
    for k in range(chips):
        for c in range(2):
            x[c * half + k * SLOT : c * half + k * SLOT + rows, :] = got[k][c]
    width = encs[0].shape[1]
    for j in range(cores):
        h = jnp.dot(x[...], encs[j][...], preferred_element_type=jnp.float32)
        pre = jnp.where(smalls[j][1:2, :] > 0.5, h[half:], h[:half]) + smalls[j][0:1, :]
        out[:, j * width : (j + 1) * width] = jnp.maximum(pre, 0.0).astype(jnp.bfloat16)


def dots(feats, decs, level, cores):
    width = decs[0].shape[1]
    total = None
    for j in range(cores):
        one = jnp.dot(
            feats[:, j * width : (j + 1) * width],
            decs[j][level],
            preferred_element_type=jnp.float32,
        )
        total = one if total is None else total + one
    return total


def own_body(cores, feats, *refs):
    decs, out = refs[:cores], refs[cores]
    out[...] = dots(feats, decs, 0, cores)


def rest_body(chips, cores, depth, rows, base, bias, *refs):
    known, decs = refs[:depth], refs[depth : depth + cores]
    outs = refs[depth + cores :]
    outs, total = outs[:-1], outs[-1]
    total[...] = base[...]
    for k in range(depth):

        @pl.when(lax.axis_index("layer") > k)
        def _():
            total[...] += dots(known[k], decs, k + 1, cores)

    outs[0][...] = total[:rows] + bias[...]
    for k in range(1, chips):
        outs[k][...] = total[k * SLOT : k * SLOT + rows].astype(jnp.bfloat16)


def sum_body(own, *refs):
    total = own[...]
    for r in refs[:-1]:
        total = total + r[...].astype(jnp.float32)
    refs[-1][0] = total.astype(jnp.bfloat16)


def local(clean_resid, corrupt_resid, enc_weight, enc_bias, dec_weight, dec_bias, patch_index):
    chips = lax.axis_size("feat")
    cores = lax.axis_size("dec")
    depth = min(REACH - 1, lax.axis_size("layer") - 1)
    width = enc_weight.shape[2]
    rows, model = clean_resid.shape[1:]
    bf16, f32 = jnp.bfloat16, jnp.float32
    any_, hbm, dma = pl.ANY, pltpu.HBM, pltpu.SemaphoreType.DMA

    both = call(
        stack_body,
        VMEM((2, rows, model), bf16),
        (hbm,) * 2,
        [far(v) for v in (clean_resid, corrupt_resid)],
        (dma((2,)),),
    )
    got = [rotated(both, "feat", k) for k in range(1, chips)]
    enc, dec, small = call(
        functools.partial(load_body, depth + 1),
        (
            VMEM((model, width), bf16),
            VMEM((depth + 1, width, model), bf16),
            VMEM((2, width), f32),
        ),
        (hbm,) * 4 + (any_,),
        [far(v) for v in (enc_weight, dec_weight, enc_bias, patch_index)] + [got[2]],
        (
            VMEM((1, width), f32),
            pltpu.SMEM(patch_index.shape[1:], jnp.int32),
            dma((depth + 4,)),
        ),
    )
    smalls = [small] + [rotated(small, "dec", j) for j in range(1, cores)]
    got = [both] + got
    encs = [enc] + [rotated(enc_weight[0], "dec", j) for j in range(1, cores)]
    decs = [dec] + [rotated(dec_weight[0], "dec", j) for j in range(1, cores)]
    feats = call(
        functools.partial(encode_body, chips, cores),
        VMEM((chips * SLOT, cores * width), bf16),
        (VMEM,) * (chips + 2 * cores),
        [near(v) for v in (*got[::-1], *smalls, *encs)],
        (VMEM((2 * chips * SLOT, model), bf16),),
        flops=4 * chips * SLOT * model * width * cores,
        moved=cores * width * model * 2,
    )
    known = [rotated(feats, "layer", o) for o in range(1, depth + 1)]
    base = call(
        functools.partial(own_body, cores),
        VMEM((chips * SLOT, model), f32),
        (VMEM,) * (1 + cores),
        [near(v) for v in (feats, *decs)],
        flops=2 * chips * SLOT * model * width * cores,
        moved=cores * width * model * 2,
    )
    parts = call(
        functools.partial(rest_body, chips, cores, depth, rows),
        (VMEM((rows, model), f32),) + (VMEM((rows, model), bf16),) * (chips - 1),
        (VMEM,) * (2 + depth + cores),
        [near(v) for v in (base, dec_bias, *known, *decs)],
        (VMEM((chips * SLOT, model), f32),),
        flops=2 * chips * SLOT * model * width * cores * depth,
        moved=cores * width * model * 2 * depth,
    )
    back = [rotated(parts[k], "feat", -k) for k in range(chips - 1, 0, -1)]
    return call(
        sum_body,
        jax.ShapeDtypeStruct((1, rows, model), bf16),
        (VMEM,) * chips,
        [near(v) for v in (parts[0], *back)],
    )


def solution(mesh):
    placed = (
        P("layer", ("grp", "feat", "dec"), None),
        P("layer", ("grp", "feat", "dec"), None),
        P("layer", None, ("feat", "dec")),
        P("layer", ("feat", "dec")),
        P("layer", None, ("feat", "dec"), None),
        P("layer", None),
        P("layer", ("feat", "dec"), None),
    )
    return jax.shard_map(
        local,
        mesh=mesh,
        in_specs=placed,
        out_specs=P("layer", ("grp", "feat", "dec"), None),
        check_vma=False,
    )
```

```python
import functools

import jax
import jax.numpy as jnp
from jax import lax
from jax.experimental import pallas as pl
from jax.experimental.pallas import tpu as pltpu
from jax.sharding import PartitionSpec as P

REACH = 3
SLOT = 16
FIRST = 0
VMEM = pltpu.VMEM
LIMIT = 48 * 1024 * 1024


def shifted(value, axis, by):
    count = lax.axis_size(axis)
    return lax.ppermute(value, axis, [(i, i + by) for i in range(count) if 0 <= i + by < count])


def rotated(value, axis, by):
    count = lax.axis_size(axis)
    return lax.ppermute(value, axis, [(i, (i + by) % count) for i in range(count)])


def paired(value, axis, by):
    count = lax.axis_size(axis)
    return lax.ppermute(value, axis, [(i, i ^ by) for i in range(count)])


def near(value):
    return pltpu.with_memory_space_constraint(value, VMEM)


def far(value):
    return pltpu.with_memory_space_constraint(value, pltpu.HBM)


def call(body, outs, spaces, args, scratch=(), flops=0, moved=0):
    return pl.pallas_call(
        body,
        out_shape=outs,
        in_specs=[pl.BlockSpec(memory_space=s) for s in spaces],
        out_specs=jax.tree.map(lambda _: pl.BlockSpec(memory_space=VMEM), outs),
        scratch_shapes=list(scratch),
        compiler_params=pltpu.CompilerParams(vmem_limit_bytes=LIMIT),
        cost_estimate=pl.CostEstimate(flops=flops, bytes_accessed=moved, transcendentals=0),
    )(*args)


def stack_body(clean, corrupt, both, sems):
    copies = [
        pltpu.make_async_copy(clean.at[0], both.at[0], sems.at[0]),
        pltpu.make_async_copy(corrupt.at[0], both.at[1], sems.at[1]),
    ]
    for c in copies:
        c.start()
    for c in copies:
        c.wait()


def load_body(levels, enc, dec, bias, picks, after, enc_out, dec_out, small, bias_v, picks_s, sems):
    copies = [
        pltpu.make_async_copy(picks.at[0], picks_s, sems.at[0]),
        pltpu.make_async_copy(bias, bias_v, sems.at[1]),
        pltpu.make_async_copy(enc.at[0], enc_out, sems.at[2]),
    ]
    copies += [
        pltpu.make_async_copy(dec.at[0, k], dec_out.at[k], sems.at[k + 3]) for k in range(levels)
    ]
    for c in copies:
        c.start()
    copies[0].wait()
    width = small.shape[1]
    lane = lax.broadcasted_iota(jnp.int32, (1, width), 1)
    mark = jnp.zeros((1, width), jnp.float32)
    for i in range(picks_s.shape[1]):
        mark = jnp.where(lane == picks_s[0, i], 1.0, mark)
    small[1:2, :] = mark
    copies[1].wait()
    small[0:1, :] = bias_v[...]
    for c in copies[2:]:
        c.wait()


def encode_body(count, cores, earlier, *refs):
    refs = refs[earlier:]
    got, refs = refs[:count], refs[count:]
    smalls, encs, (out, x) = refs[:cores], refs[cores : 2 * cores], refs[2 * cores :]
    rows = got[0].shape[1]
    half = count * SLOT
    for i in range(count):
        for c in range(2):
            x[c * half + i * SLOT : c * half + i * SLOT + rows, :] = got[i][c]
    width = encs[0].shape[1]
    for j in range(cores):
        h = jnp.dot(x[...], encs[j][...], preferred_element_type=jnp.float32)
        pre = jnp.where(smalls[j][1:2, :] > 0.5, h[half:], h[:half]) + smalls[j][0:1, :]
        feats = jnp.maximum(pre, 0.0).astype(jnp.bfloat16)
        for i in range(count):
            out[i, :, j * width : (j + 1) * width] = feats[i * SLOT : i * SLOT + rows]


def dots(feats, decs, level, x):
    width = decs[0].shape[1]
    count, rows = feats.shape[:2]
    for i in range(count):
        x[i * SLOT : i * SLOT + rows, :] = feats[i]
    total = None
    for j, dec in enumerate(decs):
        one = jnp.dot(
            x[:, j * width : (j + 1) * width], dec[level], preferred_element_type=jnp.float32
        )
        total = one if total is None else total + one
    return total


def own_body(cores, feats, *refs):
    decs, (out, x) = refs[:cores], refs[-2:]
    out[...] = dots(feats, decs, 0, x)


def rest_body(cores, depth, slots, rows, base, bias, *refs):
    known, decs = refs[:depth], refs[depth : depth + cores]
    outs, (total, x) = refs[depth + cores : -2], refs[-2:]
    total[...] = base[...]
    for k in range(depth):

        @pl.when(lax.axis_index("layer") > k)
        def _():
            total[...] += dots(known[k], decs, k + 1, x)

    for i, slot in enumerate(slots):
        part = total[i * SLOT : i * SLOT + rows]
        outs[i][...] = part + bias[...] if slot == 0 else part.astype(jnp.bfloat16)


def sum_body(own, *refs):
    total = own[...]
    for r in refs[:-1]:
        total = total + r[...].astype(jnp.float32)
    refs[-1][0] = total.astype(jnp.bfloat16)


def local(clean_resid, corrupt_resid, enc_weight, enc_bias, dec_weight, dec_bias, patch_index):
    chips = lax.axis_size("feat")
    cores = lax.axis_size("dec")
    depth = min(REACH - 1, lax.axis_size("layer") - 1)
    width = enc_weight.shape[2]
    rows, model = clean_resid.shape[1:]
    bf16, f32 = jnp.bfloat16, jnp.float32
    any_, hbm, dma = pl.ANY, pltpu.HBM, pltpu.SemaphoreType.DMA

    both = call(
        stack_body,
        VMEM((2, rows, model), bf16),
        (hbm,) * 2,
        [far(v) for v in (clean_resid, corrupt_resid)],
        (dma((2,)),),
    )
    relayed = [k for k in range(2, chips) if k % 2]
    got = [both] + [None if k in relayed else paired(both, "feat", k) for k in range(1, chips)]
    enc, dec, small = call(
        functools.partial(load_body, depth + 1),
        (
            VMEM((model, width), bf16),
            VMEM((depth + 1, width, model), bf16),
            VMEM((2, width), f32),
        ),
        (hbm,) * 4 + (any_,),
        [far(v) for v in (enc_weight, dec_weight, enc_bias, patch_index)] + [got[1]],
        (
            VMEM((1, width), f32),
            pltpu.SMEM(patch_index.shape[1:], jnp.int32),
            dma((depth + 4,)),
        ),
    )
    if relayed:
        *held, small = lax.optimization_barrier((*[got[k - 1] for k in relayed], small))
        for k, v in zip(relayed, held):
            got[k - 1] = v
            got[k] = paired(v, "feat", 1)
    smalls = [small] + [rotated(small, "dec", j) for j in range(1, cores)]
    encs = [enc] + [rotated(enc_weight[0], "dec", j) for j in range(1, cores)]
    decs = [dec] + [rotated(dec_weight[0], "dec", j) for j in range(1, cores)]
    wide = cores * width
    parts = [None] * chips
    before_encode = before_own = ()
    direct = [k for k in range(chips) if k not in relayed]
    for slots in filter(None, (direct, relayed)):
        n = len(slots)
        feats = call(
            functools.partial(encode_body, n, cores, len(before_encode)),
            VMEM((n, rows, wide), bf16),
            (any_,) * len(before_encode) + (VMEM,) * (n + 2 * cores),
            [near(v) for v in (*before_encode, *[got[k] for k in slots], *smalls, *encs)],
            (VMEM((2 * n * SLOT, model), bf16),),
            flops=4 * n * SLOT * model * wide,
            moved=wide * model * 2,
        )
        known = [rotated(feats, "layer", o) for o in range(1, depth + 1)]
        base = call(
            functools.partial(own_body, cores),
            VMEM((n * SLOT, model), f32),
            (VMEM,) * (1 + cores) + (any_,) * len(before_own),
            [near(v) for v in (feats, *decs, *before_own)],
            (VMEM((n * SLOT, wide), bf16),),
            flops=2 * n * SLOT * model * wide,
            moved=wide * model * 2,
        )
        outs = call(
            functools.partial(rest_body, cores, depth, slots, rows),
            tuple(VMEM((rows, model), bf16 if k else f32) for k in slots),
            (VMEM,) * (2 + depth + cores),
            [near(v) for v in (base, dec_bias, *known, *decs)],
            (VMEM((n * SLOT, model), f32), VMEM((n * SLOT, wide), bf16)),
            flops=2 * n * SLOT * model * wide * depth,
            moved=wide * model * 2 * depth,
        )
        for k, out in zip(slots, outs):
            parts[k] = out
        before_encode, before_own = (base,), (outs[-1],)
    if relayed:
        parts[1], parts[-1] = lax.optimization_barrier((parts[1], parts[-1]))
    back = [paired(parts[k], "feat", k) for k in range(chips - 1, 0, -1)]
    return call(
        sum_body,
        jax.ShapeDtypeStruct((1, rows, model), bf16),
        (VMEM,) * chips,
        [near(v) for v in (parts[0], *back)],
    )


def solution(mesh):
    placed = (
        P("layer", ("grp", "feat", "dec"), None),
        P("layer", ("grp", "feat", "dec"), None),
        P("layer", None, ("feat", "dec")),
        P("layer", ("feat", "dec")),
        P("layer", None, ("feat", "dec"), None),
        P("layer", None),
        P("layer", ("feat", "dec"), None),
    )
    return jax.shard_map(
        local,
        mesh=mesh,
        in_specs=placed,
        out_specs=P("layer", ("grp", "feat", "dec"), None),
        check_vma=False,
    )
```

```python
import functools

import jax
import jax.numpy as jnp
from jax import lax
from jax.experimental import pallas as pl
from jax.experimental.pallas import tpu as pltpu
from jax.sharding import PartitionSpec as P

REACH = 3
SLOT = 16
FIRST = 0
VMEM = pltpu.VMEM
LIMIT = 48 * 1024 * 1024


def shifted(value, axis, by):
    count = lax.axis_size(axis)
    return lax.ppermute(value, axis, [(i, i + by) for i in range(count) if 0 <= i + by < count])


def rotated(value, axis, by):
    count = lax.axis_size(axis)
    return lax.ppermute(value, axis, [(i, (i + by) % count) for i in range(count)])


def paired(value, axis, by):
    count = lax.axis_size(axis)
    return lax.ppermute(value, axis, [(i, i ^ by) for i in range(count)])


def near(value):
    return pltpu.with_memory_space_constraint(value, VMEM)


def far(value):
    return pltpu.with_memory_space_constraint(value, pltpu.HBM)


def call(body, outs, spaces, args, scratch=(), flops=0, moved=0):
    return pl.pallas_call(
        body,
        out_shape=outs,
        in_specs=[pl.BlockSpec(memory_space=s) for s in spaces],
        out_specs=jax.tree.map(lambda _: pl.BlockSpec(memory_space=VMEM), outs),
        scratch_shapes=list(scratch),
        compiler_params=pltpu.CompilerParams(vmem_limit_bytes=LIMIT),
        cost_estimate=pl.CostEstimate(flops=flops, bytes_accessed=moved, transcendentals=0),
    )(*args)


def stack_body(clean, corrupt, both, sems):
    copies = [
        pltpu.make_async_copy(clean.at[0], both.at[0], sems.at[0]),
        pltpu.make_async_copy(corrupt.at[0], both.at[1], sems.at[1]),
    ]
    for c in copies:
        c.start()
    for c in copies:
        c.wait()


def load_body(levels, enc, dec, bias, picks, after, enc_out, dec_out, small, bias_v, picks_s, sems):
    copies = [
        pltpu.make_async_copy(picks.at[0], picks_s, sems.at[0]),
        pltpu.make_async_copy(bias, bias_v, sems.at[1]),
        pltpu.make_async_copy(enc.at[0], enc_out, sems.at[2]),
    ]
    copies += [
        pltpu.make_async_copy(dec.at[0, k], dec_out.at[k], sems.at[k + 3]) for k in range(levels)
    ]
    for c in copies:
        c.start()
    copies[0].wait()
    width = small.shape[1]
    lane = lax.broadcasted_iota(jnp.int32, (1, width), 1)
    mark = jnp.zeros((1, width), jnp.float32)
    for i in range(picks_s.shape[1]):
        mark = jnp.where(lane == picks_s[0, i], 1.0, mark)
    small[1:2, :] = mark
    copies[1].wait()
    small[0:1, :] = bias_v[...]
    for c in copies[2:]:
        c.wait()


def encode_body(count, cores, earlier, *refs):
    refs = refs[earlier:]
    got, refs = refs[:count], refs[count:]
    smalls, encs, (out, x) = refs[:cores], refs[cores : 2 * cores], refs[2 * cores :]
    rows = got[0].shape[1]
    half = count * SLOT
    for i in range(count):
        for c in range(2):
            x[c * half + i * SLOT : c * half + i * SLOT + rows, :] = got[i][c]
    width = encs[0].shape[1]
    for j in range(cores):
        h = jnp.dot(x[...], encs[j][...], preferred_element_type=jnp.float32)
        pre = jnp.where(smalls[j][1:2, :] > 0.5, h[half:], h[:half]) + smalls[j][0:1, :]
        feats = jnp.maximum(pre, 0.0).astype(jnp.bfloat16)
        for i in range(count):
            out[i, :, j * width : (j + 1) * width] = feats[i * SLOT : i * SLOT + rows]


def dots(feats, decs, level, x):
    width = decs[0].shape[1]
    count, rows = feats.shape[:2]
    for i in range(count):
        x[i * SLOT : i * SLOT + rows, :] = feats[i]
    total = None
    for j, dec in enumerate(decs):
        one = jnp.dot(
            x[:, j * width : (j + 1) * width], dec[level], preferred_element_type=jnp.float32
        )
        total = one if total is None else total + one
    return total


def own_body(cores, feats, *refs):
    decs, (out, x) = refs[:cores], refs[cores:]
    out[...] = dots(feats, decs, 0, x)


def rest_body(cores, depth, extra, slots, rows, base, bias, *refs):
    known, decs = refs[:depth], refs[depth : depth + cores]
    outs, (total, x) = refs[depth + cores + extra : -2], refs[-2:]
    total[...] = base[...]
    for k in range(depth):

        @pl.when(lax.axis_index("layer") > k)
        def _():
            total[...] += dots(known[k], decs, k + 1, x)

    for i, slot in enumerate(slots):
        part = total[i * SLOT : i * SLOT + rows]
        outs[i][...] = part + bias[...] if slot == 0 else part.astype(jnp.bfloat16)


def sum_body(own, *refs):
    total = own[...]
    for r in refs[:-1]:
        total = total + r[...].astype(jnp.float32)
    refs[-1][0] = total.astype(jnp.bfloat16)


def local(clean_resid, corrupt_resid, enc_weight, enc_bias, dec_weight, dec_bias, patch_index):
    chips = lax.axis_size("feat")
    cores = lax.axis_size("dec")
    depth = min(REACH - 1, lax.axis_size("layer") - 1)
    width = enc_weight.shape[2]
    rows, model = clean_resid.shape[1:]
    bf16, f32 = jnp.bfloat16, jnp.float32
    any_, hbm, dma = pl.ANY, pltpu.HBM, pltpu.SemaphoreType.DMA

    both = call(
        stack_body,
        VMEM((2, rows, model), bf16),
        (hbm,) * 2,
        [far(v) for v in (clean_resid, corrupt_resid)],
        (dma((2,)),),
    )
    relayed = [k for k in range(2, chips) if k % 2]
    got = [both] + [None if k in relayed else paired(both, "feat", k) for k in range(1, chips)]
    enc, dec, small = call(
        functools.partial(load_body, depth + 1),
        (
            VMEM((model, width), bf16),
            VMEM((depth + 1, width, model), bf16),
            VMEM((2, width), f32),
        ),
        (hbm,) * 4 + (any_,),
        [far(v) for v in (enc_weight, dec_weight, enc_bias, patch_index)] + [got[1]],
        (
            VMEM((1, width), f32),
            pltpu.SMEM(patch_index.shape[1:], jnp.int32),
            dma((depth + 4,)),
        ),
    )
    if relayed:
        *held, small = lax.optimization_barrier((*[got[k - 1] for k in relayed], small))
        for k, v in zip(relayed, held):
            got[k - 1] = v
            got[k] = paired(v, "feat", 1)
    smalls = [small] + [rotated(small, "dec", j) for j in range(1, cores)]
    encs = [enc] + [rotated(enc_weight[0], "dec", j) for j in range(1, cores)]
    decs = [dec] + [rotated(dec_weight[0], "dec", j) for j in range(1, cores)]
    wide = cores * width
    parts = [None] * chips
    before_encode = ()
    groups = []
    direct = [k for k in range(chips) if k not in relayed]
    for slots in filter(None, (direct, relayed)):
        n = len(slots)
        feats = call(
            functools.partial(encode_body, n, cores, len(before_encode)),
            VMEM((n, rows, wide), bf16),
            (any_,) * len(before_encode) + (VMEM,) * (n + 2 * cores),
            [near(v) for v in (*before_encode, *[got[k] for k in slots], *smalls, *encs)],
            (VMEM((2 * n * SLOT, model), bf16),),
            flops=4 * n * SLOT * model * wide,
            moved=wide * model * 2,
        )
        known = [rotated(feats, "layer", o) for o in range(1, depth + 1)]
        base = call(
            functools.partial(own_body, cores),
            VMEM((n * SLOT, model), f32),
            (VMEM,) * (1 + cores),
            [near(v) for v in (feats, *decs)],
            (VMEM((n * SLOT, wide), bf16),),
            flops=2 * n * SLOT * model * wide,
            moved=wide * model * 2,
        )
        before_encode = (base,)
        groups.append((slots, known, base))
    for g, (slots, known, base) in enumerate(groups):
        n = len(slots)
        later = tuple(other for _, _, other in groups[g + 1 :])
        outs = call(
            functools.partial(rest_body, cores, depth, len(later), slots, rows),
            tuple(VMEM((rows, model), bf16 if k else f32) for k in slots),
            (VMEM,) * (2 + depth + cores) + (any_,) * len(later),
            [near(v) for v in (base, dec_bias, *known, *decs, *later)],
            (VMEM((n * SLOT, model), f32), VMEM((n * SLOT, wide), bf16)),
            flops=2 * n * SLOT * model * wide * depth,
            moved=wide * model * 2 * depth,
        )
        for k, out in zip(slots, outs):
            parts[k] = out
    if relayed:
        parts[1], parts[-1] = lax.optimization_barrier((parts[1], parts[-1]))
    back = [paired(parts[k], "feat", k) for k in range(chips - 1, 0, -1)]
    return call(
        sum_body,
        jax.ShapeDtypeStruct((1, rows, model), bf16),
        (VMEM,) * chips,
        [near(v) for v in (parts[0], *back)],
    )


def solution(mesh):
    placed = (
        P("layer", ("grp", "feat", "dec"), None),
        P("layer", ("grp", "feat", "dec"), None),
        P("layer", None, ("feat", "dec")),
        P("layer", ("feat", "dec")),
        P("layer", None, ("feat", "dec"), None),
        P("layer", None),
        P("layer", ("feat", "dec"), None),
    )
    return jax.shard_map(
        local,
        mesh=mesh,
        in_specs=placed,
        out_specs=P("layer", ("grp", "feat", "dec"), None),
        check_vma=False,
    )
```

```python
import functools

import jax
import jax.numpy as jnp
from jax import lax
from jax.experimental import pallas as pl
from jax.experimental.pallas import tpu as pltpu
from jax.sharding import PartitionSpec as P

REACH = 3
SLOT = 16
FIRST = 0
VMEM = pltpu.VMEM
LIMIT = 48 * 1024 * 1024


def shifted(value, axis, by):
    count = lax.axis_size(axis)
    return lax.ppermute(value, axis, [(i, i + by) for i in range(count) if 0 <= i + by < count])


def rotated(value, axis, by):
    count = lax.axis_size(axis)
    return lax.ppermute(value, axis, [(i, (i + by) % count) for i in range(count)])


def paired(value, axis, by):
    count = lax.axis_size(axis)
    return lax.ppermute(value, axis, [(i, i ^ by) for i in range(count)])


def near(value):
    return pltpu.with_memory_space_constraint(value, VMEM)


def far(value):
    return pltpu.with_memory_space_constraint(value, pltpu.HBM)


def call(body, outs, spaces, args, scratch=(), flops=0, moved=0):
    return pl.pallas_call(
        body,
        out_shape=outs,
        in_specs=[pl.BlockSpec(memory_space=s) for s in spaces],
        out_specs=jax.tree.map(lambda _: pl.BlockSpec(memory_space=VMEM), outs),
        scratch_shapes=list(scratch),
        compiler_params=pltpu.CompilerParams(vmem_limit_bytes=LIMIT),
        cost_estimate=pl.CostEstimate(flops=flops, bytes_accessed=moved, transcendentals=0),
    )(*args)


def stack_body(clean, corrupt, both, sems):
    copies = [
        pltpu.make_async_copy(clean.at[0], both.at[0], sems.at[0]),
        pltpu.make_async_copy(corrupt.at[0], both.at[1], sems.at[1]),
    ]
    for c in copies:
        c.start()
    for c in copies:
        c.wait()


def load_body(levels, enc, dec, bias, picks, after, enc_out, dec_out, small, bias_v, picks_s, sems):
    copies = [
        pltpu.make_async_copy(picks.at[0], picks_s, sems.at[0]),
        pltpu.make_async_copy(bias, bias_v, sems.at[1]),
        pltpu.make_async_copy(enc.at[0], enc_out, sems.at[2]),
    ]
    copies += [
        pltpu.make_async_copy(dec.at[0, k], dec_out.at[k], sems.at[k + 3]) for k in range(levels)
    ]
    for c in copies:
        c.start()
    copies[0].wait()
    width = small.shape[1]
    lane = lax.broadcasted_iota(jnp.int32, (1, width), 1)
    mark = jnp.zeros((1, width), jnp.float32)
    for i in range(picks_s.shape[1]):
        mark = jnp.where(lane == picks_s[0, i], 1.0, mark)
    small[1:2, :] = mark
    copies[1].wait()
    small[0:1, :] = bias_v[...]
    for c in copies[2:]:
        c.wait()


def encode_body(count, cores, earlier, *refs):
    refs = refs[earlier:]
    got, refs = refs[:count], refs[count:]
    smalls, encs, (out, x) = refs[:cores], refs[cores : 2 * cores], refs[2 * cores :]
    rows = got[0].shape[1]
    half = count * SLOT
    for i in range(count):
        for c in range(2):
            x[c * half + i * SLOT : c * half + i * SLOT + rows, :] = got[i][c]
    width = encs[0].shape[1]
    for j in range(cores):
        h = jnp.dot(x[...], encs[j][...], preferred_element_type=jnp.float32)
        pre = jnp.where(smalls[j][1:2, :] > 0.5, h[half:], h[:half]) + smalls[j][0:1, :]
        feats = jnp.maximum(pre, 0.0).astype(jnp.bfloat16)
        for i in range(count):
            out[i, :, j * width : (j + 1) * width] = feats[i * SLOT : i * SLOT + rows]


def dots(feats, decs, level, x):
    width = decs[0].shape[1]
    count, rows = feats.shape[:2]
    for i in range(count):
        x[i * SLOT : i * SLOT + rows, :] = feats[i]
    total = None
    for j, dec in enumerate(decs):
        one = jnp.dot(
            x[:, j * width : (j + 1) * width], dec[level], preferred_element_type=jnp.float32
        )
        total = one if total is None else total + one
    return total


def own_body(cores, feats, *refs):
    decs, (out, x) = refs[:cores], refs[cores:]
    out[...] = dots(feats, decs, 0, x)


def rest_body(cores, depth, extra, slots, rows, base, bias, *refs):
    known, decs = refs[:depth], refs[depth : depth + cores]
    outs, (total, x) = refs[depth + cores + extra : -2], refs[-2:]
    total[...] = base[...]
    for k in range(depth):

        @pl.when(lax.axis_index("layer") > k)
        def _():
            total[...] += dots(known[k], decs, k + 1, x)

    for i, slot in enumerate(slots):
        part = total[i * SLOT : i * SLOT + rows]
        outs[i][...] = part + bias[...] if slot == 0 else part.astype(jnp.bfloat16)


def sum_body(own, *refs):
    total = own[...]
    for r in refs[:-1]:
        total = total + r[...].astype(jnp.float32)
    refs[-1][0] = total.astype(jnp.bfloat16)


def local(clean_resid, corrupt_resid, enc_weight, enc_bias, dec_weight, dec_bias, patch_index):
    chips = lax.axis_size("feat")
    cores = lax.axis_size("dec")
    depth = min(REACH - 1, lax.axis_size("layer") - 1)
    width = enc_weight.shape[2]
    rows, model = clean_resid.shape[1:]
    bf16, f32 = jnp.bfloat16, jnp.float32
    any_, hbm, dma = pl.ANY, pltpu.HBM, pltpu.SemaphoreType.DMA

    both = call(
        stack_body,
        VMEM((2, rows, model), bf16),
        (hbm,) * 2,
        [far(v) for v in (clean_resid, corrupt_resid)],
        (dma((2,)),),
    )
    relayed = [k for k in range(2, chips) if k % 2]
    got = [both] + [None if k in relayed else paired(both, "feat", k) for k in range(1, chips)]
    swapped = [rotated(enc_weight[0], "dec", j) for j in range(1, cores)]
    enc, dec, small = call(
        functools.partial(load_body, depth + 1),
        (
            VMEM((model, width), bf16),
            VMEM((depth + 1, width, model), bf16),
            VMEM((2, width), f32),
        ),
        (hbm,) * 4 + (any_,),
        [far(v) for v in (enc_weight, dec_weight, enc_bias, patch_index)] + [swapped[0]],
        (
            VMEM((1, width), f32),
            pltpu.SMEM(patch_index.shape[1:], jnp.int32),
            dma((depth + 4,)),
        ),
    )
    if relayed:
        *held, small = lax.optimization_barrier((*[got[k - 1] for k in relayed], small))
        for k, v in zip(relayed, held):
            got[k - 1] = v
            got[k] = paired(v, "feat", 1)
    smalls = [small] + [rotated(small, "dec", j) for j in range(1, cores)]
    encs = [enc] + swapped
    decs = [dec] + [rotated(dec_weight[0], "dec", j) for j in range(1, cores)]
    wide = cores * width
    parts = [None] * chips
    before_encode = ()
    groups = []
    direct = [k for k in range(chips) if k not in relayed]
    for slots in filter(None, (direct, relayed)):
        n = len(slots)
        feats = call(
            functools.partial(encode_body, n, cores, len(before_encode)),
            VMEM((n, rows, wide), bf16),
            (any_,) * len(before_encode) + (VMEM,) * (n + 2 * cores),
            [near(v) for v in (*before_encode, *[got[k] for k in slots], *smalls, *encs)],
            (VMEM((2 * n * SLOT, model), bf16),),
            flops=4 * n * SLOT * model * wide,
            moved=wide * model * 2,
        )
        known = [rotated(feats, "layer", o) for o in range(1, depth + 1)]
        base = call(
            functools.partial(own_body, cores),
            VMEM((n * SLOT, model), f32),
            (VMEM,) * (1 + cores),
            [near(v) for v in (feats, *decs)],
            (VMEM((n * SLOT, wide), bf16),),
            flops=2 * n * SLOT * model * wide,
            moved=wide * model * 2,
        )
        before_encode = (base,)
        groups.append((slots, known, base))
    for g, (slots, known, base) in enumerate(groups):
        n = len(slots)
        later = tuple(other for _, _, other in groups[g + 1 :])
        outs = call(
            functools.partial(rest_body, cores, depth, len(later), slots, rows),
            tuple(VMEM((rows, model), bf16 if k else f32) for k in slots),
            (VMEM,) * (2 + depth + cores) + (any_,) * len(later),
            [near(v) for v in (base, dec_bias, *known, *decs, *later)],
            (VMEM((n * SLOT, model), f32), VMEM((n * SLOT, wide), bf16)),
            flops=2 * n * SLOT * model * wide * depth,
            moved=wide * model * 2 * depth,
        )
        for k, out in zip(slots, outs):
            parts[k] = out
    if relayed:
        parts[1], parts[-1] = lax.optimization_barrier((parts[1], parts[-1]))
    back = [paired(parts[k], "feat", k) for k in range(chips - 1, 0, -1)]
    return call(
        sum_body,
        jax.ShapeDtypeStruct((1, rows, model), bf16),
        (VMEM,) * chips,
        [near(v) for v in (parts[0], *back)],
    )


def solution(mesh):
    placed = (
        P("layer", ("grp", "feat", "dec"), None),
        P("layer", ("grp", "feat", "dec"), None),
        P("layer", None, ("feat", "dec")),
        P("layer", ("feat", "dec")),
        P("layer", None, ("feat", "dec"), None),
        P("layer", None),
        P("layer", ("feat", "dec"), None),
    )
    return jax.shard_map(
        local,
        mesh=mesh,
        in_specs=placed,
        out_specs=P("layer", ("grp", "feat", "dec"), None),
        check_vma=False,
    )
```
